128 devices in a mesh: group: 16 (over x, y), span: 8 (over z, core).
Axes of the slice: x: 4, y: 4, z: 4, core: 2. Of those that a mesh axis runs over, the one named last changes fastest.
Arguments:
- embeddings: float32 [49152, 1024], P(('group', 'span')), may hold values from -100 to 100
- cluster_ids: int32 [49152, 1], P(('group', 'span')), may hold values from 0 to 47; in each aligned block of 384 rows (0 to 383, 384 to 767, ...) at most 24 rows name the same one
- order: int32 [49152], P(('group', 'span')), may hold values from 0 to 49151, each once
Outputs:
- nearest: float32 [49152], P(('group', 'span'))
The draws below stay inside these ranges and needn't reach their ends.
Inputs may be any that keep to these rules, and one draw needn't show every extreme that they name: `cluster_ids`: in the rows of one device no cluster appears more than 24 times, and some cluster appears exactly 24 times. `order`: each number appears once.
All inputs are finite; a program needn't handle non-finite values.
Results may differ from the reference program's by a relative error of at most 0.00048.
Values may be sent and summed in bfloat16 or wider, within the bound.
No kernel may reach another device: no remote copies, remote signals or barrier semaphores. Data moves between devices by JAX's collectives and lax.ppermute only.
A program may use at most 128 MiB of HBM per device.

```python
import math
import jax
import jax.numpy as jnp
import numpy as np
from jax import lax

D = 1024
CLUSTERS = 48
ROWS_DEV = 384
MOST = 24
ROWS = 49152


def draw_embeddings(key, part):
    key = jax.random.fold_in(key, 11)
    key_pool, key_pick, key_mix, key_noise, key_scale = jax.random.split(key, 5)
    pool_size = ROWS // 64
    pool = jax.random.truncated_normal(key_pool, -4.0, 4.0, (pool_size, D), jnp.float32)
    picked = jax.random.randint(key_pick, (ROWS,), 0, pool_size)
    mixing = jax.random.uniform(key_mix, (ROWS, 1), jnp.float32, 0.0, 1.5)
    noise = jax.random.truncated_normal(key_noise, -4.0, 4.0, (ROWS, D), jnp.float32)
    scales = jnp.exp(jax.random.uniform(key_scale, (ROWS, 1), jnp.float32, 0.0, 2.3))
    values = (pool[picked] * mixing + noise) * scales
    return values.astype(jnp.float32)


def assign_block(rng, own, number, rows, number_of, top, reach, slope):
    ranking = jax.random.permutation(rng, number_of)
    packed, usual = load_shares(number_of, rows * top, reach, slope, True), load_shares(number_of, rows * top, reach, slope, False)
    places = jnp.arange(number_of)

    def named(sizes, turn):
        used = int((sizes > 0).sum())
        fixed = max(1, used // 4)
        passed = fixed + (places - fixed + turn * (used - fixed)) % max(1, number_of - fixed)
        return jnp.zeros((number_of,), jnp.int32).at[ranking[jnp.where(places < fixed, places, passed)]].set(jnp.asarray(sizes, jnp.int32))

    sizes = jnp.where(number % 4 == 0, named(packed, number // 4), named(usual, number - number // 4 - 1))
    mixed = jax.random.permutation(jax.random.fold_in(own, 3), number_of)
    giver, taker = mixed[0:number_of // 2 * 2:2], mixed[1:number_of // 2 * 2:2]
    room = jnp.minimum(sizes[giver] - 1, reach - sizes[taker]) // 2
    room = jnp.where((giver == ranking[0]) | (taker == ranking[0]) | (sizes[taker] == 0), 0, jnp.maximum(room, 0))
    passed = jax.random.randint(jax.random.fold_in(own, 4), (number_of // 2,), 0, 1 << 20) % (room + 1)
    sizes = sizes.at[giver].add(-passed).at[taker].add(passed)
    labels = jnp.searchsorted(jnp.cumsum(sizes), jnp.arange(rows * top), side="right").astype(jnp.int32)
    table = labels.reshape(top, rows).T
    table = table[jax.random.permutation(jax.random.fold_in(own, 1), rows)]
    turn = jax.random.randint(jax.random.fold_in(own, 2), (rows, 1), 0, top)
    return jnp.take_along_axis(table, (jnp.arange(top)[None, :] + turn) % top, axis=1)


def load_shares(count, total, most, slope, full):
    weights = [(1 << 20) // math.isqrt(rank ** slope) + 1 for rank in range(1, count + 1)]
    largest = most if full else min(most, max(-(-total // count), total * weights[0] // sum(weights)))
    least = 1 if total - largest >= count - 1 else 0
    counts, surplus = [largest] + [least] * (count - 1), total - largest - least * (count - 1)
    while surplus > 0:
        movable = [i for i in range(1, count) if counts[i] < largest] or [i for i in range(1, count) if counts[i] < most]
        whole, left = sum([weights[i] for i in movable]), surplus
        for i in movable:
            addition = min(most - counts[i], max(1, left * weights[i] // whole), surplus)
            counts[i] = counts[i] + addition
            surplus = surplus - addition
    return np.array(counts)


def setup_inputs(seed: int = 0) -> dict:
    streams_of = jax.random.split(jax.random.key(seed), 4)
    embeddings = draw_embeddings(jax.random.fold_in(streams_of[3], 71), 0)
    cluster_ids_keys = jax.random.split(jax.random.fold_in(streams_of[1], 1), ROWS // ROWS_DEV)
    cluster_ids_turns = jax.random.permutation(jax.random.fold_in(streams_of[1], 3), ROWS // ROWS_DEV)
    cluster_ids = jax.vmap(lambda own, number: assign_block(jax.random.fold_in(streams_of[1], 2), own, number, ROWS_DEV, CLUSTERS, 1, MOST, 2))(cluster_ids_keys, cluster_ids_turns).reshape((ROWS, 1))
    order = jax.random.permutation(streams_of[2], ROWS).astype(jnp.int32)
    return {"embeddings": embeddings, "cluster_ids": cluster_ids, "order": order}


def reference(embeddings, cluster_ids, order):
    unit = (embeddings * lax.rsqrt(lax.optimization_barrier(jnp.sum(embeddings * embeddings, axis=1, keepdims=True)) + 1e-06)).astype(jnp.bfloat16)
    cluster = cluster_ids[:, 0]
    permuted = jnp.argsort(cluster, stable=True).astype(jnp.int32)
    sorted_units = unit[permuted].astype(jnp.float32)
    sorted_cluster = cluster[permuted]
    sorted_order = order[permuted]
    margin = ROWS // ROWS_DEV * MOST
    padded_units = jnp.concatenate([jnp.zeros((margin, D), jnp.float32), sorted_units, jnp.zeros((margin, D), jnp.float32)], axis=0)
    padded_cluster = jnp.concatenate([jnp.full((margin,), -1, jnp.int32), sorted_cluster, jnp.full((margin,), -1, jnp.int32)])
    padded_order = jnp.concatenate([jnp.zeros((margin,), jnp.int32), sorted_order, jnp.zeros((margin,), jnp.int32)])
    block_rows = 512

    def one_block(index):
        start = (index * block_rows).astype(jnp.int32)
        queries = lax.dynamic_slice_in_dim(sorted_units, start, block_rows, 0)
        query_cluster = lax.dynamic_slice_in_dim(sorted_cluster, start, block_rows, 0)
        query_order = lax.dynamic_slice_in_dim(sorted_order, start, block_rows, 0)
        keys = lax.dynamic_slice_in_dim(padded_units, start, block_rows + 2 * margin, 0)
        key_cluster = lax.dynamic_slice_in_dim(padded_cluster, start, block_rows + 2 * margin, 0)
        key_order = lax.dynamic_slice_in_dim(padded_order, start, block_rows + 2 * margin, 0)
        scores = jnp.dot(queries, keys.T, precision=lax.Precision.HIGHEST, preferred_element_type=jnp.float32)
        allowed = (query_cluster[:, None] == key_cluster[None, :]) & (key_order[None, :] < query_order[:, None])
        return lax.optimization_barrier(jnp.max(jnp.where(allowed, scores, jnp.float32(-1.0)), axis=1))
    blocks = ROWS // block_rows
    results = lax.map(one_block, jnp.arange(blocks, dtype=jnp.int32)).reshape(ROWS)
    return jnp.zeros((ROWS,), jnp.float32).at[permuted].set(results)
```

```python
import jax
import jax.numpy as jnp
from jax import lax
from jax.experimental import pallas as pl
from jax.experimental.pallas import tpu as pltpu
from jax.sharding import Mesh, PartitionSpec as P

CLUSTERS = 48
MOST = 24
WIDTH = 1024
ROWS = 384
CHIPS = 64
PLANES = 4
USED = 3
BLOCKS = WIDTH // 128
CHUNK = BLOCKS * MOST + 8
HALF = CHIPS * MOST
TOP = 65535
LOW = 64
F32 = jnp.float32
BF16 = jnp.bfloat16
AXES = ("x", "y", "z", "c")
CHIP_AXES = ("x", "y", "z")


def iota(shape, dim):
    return lax.broadcasted_iota(jnp.int32, shape, dim)


def chunk_of(cluster):
    return cluster // USED * PLANES + cluster % USED


def prepare(emb_ref, cluster_ref, order_ref, send_ref, place_ref):
    cluster = cluster_ref[...]
    hot = (iota((CLUSTERS, ROWS), 0) == cluster).astype(BF16)
    before = (iota((ROWS, ROWS), 0) < iota((ROWS, ROWS), 1)).astype(BF16)
    counts = jnp.dot(hot, before, preferred_element_type=F32)
    rank = jnp.sum(counts * hot.astype(F32), axis=0, keepdims=True).astype(jnp.int32)
    slot = cluster * MOST + rank
    place_ref[...] = slot

    late = TOP - order_ref[...]
    high = (late >> 8).astype(F32)
    low = (late & 255).astype(F32)
    lane = iota((128, ROWS), 0)
    coded = jnp.where(lane == rank, high, 0.0) + jnp.where(lane == rank + LOW, low, 0.0)
    orders = lax.dot_general(
        hot, coded.astype(BF16), (((1,), (1,)), ((), ())), preferred_element_type=F32
    )

    emb = emb_ref[...]
    unit = (emb * lax.rsqrt(jnp.sum(emb * emb, axis=1, keepdims=True) + 1e-06)).astype(BF16)
    step = 16
    for part in range(CLUSTERS // step):
        rows = step * MOST
        pick = (iota((rows, ROWS), 0) + part * rows == slot).astype(BF16)
        taken = jnp.dot(pick, unit, preferred_element_type=F32).astype(BF16)
        for one in range(step):
            cluster_id = part * step + one
            to = chunk_of(cluster_id)
            for block in range(BLOCKS):
                send_ref[to, block * MOST : (block + 1) * MOST, :] = taken[
                    one * MOST : (one + 1) * MOST, block * 128 : (block + 1) * 128
                ]
            send_ref[to, BLOCKS * MOST : CHUNK, :] = jnp.broadcast_to(
                orders[cluster_id : cluster_id + 1, :], (8, 128)
            ).astype(BF16)


def key_lateness(got_ref):
    tile = got_ref[:, BLOCKS * MOST : CHUNK, :].astype(F32)
    wide = jnp.concatenate([tile, tile, tile], axis=1)
    row = iota((1, MOST, 128), 1)
    lane = iota((1, MOST, 128), 2)
    weight = jnp.where(lane == row, 256.0, 0.0) + jnp.where(lane == row + LOW, 1.0, 0.0)
    return jnp.sum((wide * weight).reshape(HALF, 128), axis=1, keepdims=True)


def unpack(got_ref, rows_ref):
    for block in range(BLOCKS):
        rows_ref[:, block * 128 : (block + 1) * 128] = got_ref[
            :, block * MOST : (block + 1) * MOST, :
        ].reshape(HALF, 128)


def best_scores(keys_ref, late_ref, queries, query_late):
    step = 256

    def body(index, best):
        start = pl.multiple_of(index * step, step)
        scores = lax.dot_general(
            keys_ref[pl.ds(start, step), :], queries, (((1,), (1,)), ((), ())),
            preferred_element_type=F32,
        )
        kept = jnp.where(late_ref[pl.ds(start, step), :] > query_late, scores, -1.0)
        return jnp.maximum(best, jnp.max(kept.reshape(step // 8, 8, HALF), axis=0))

    return lax.fori_loop(0, HALF // step, body, jnp.full((8, HALF), -1.0, F32))


def own_scores(got_ref, rows_ref, query_late_ref, best_ref, late_ref):
    unpack(got_ref, rows_ref)
    late = key_lateness(got_ref)
    late_ref[...] = late
    query_late = jnp.transpose(jnp.broadcast_to(late, (HALF, 128)))[0:1, :]
    query_late_ref[...] = query_late
    best_ref[...] = best_scores(rows_ref, late_ref, rows_ref[...], query_late)


def other_scores(got_ref, rows_ref, query_late_ref, best_ref, back_ref, keys_ref, late_ref):
    unpack(got_ref, keys_ref)
    late_ref[...] = key_lateness(got_ref)
    best = best_scores(keys_ref, late_ref, rows_ref[...], query_late_ref[...])
    best = jnp.max(jnp.maximum(best, best_ref[...]), axis=0, keepdims=True)
    column = iota((CHIPS, HALF), 1)
    source = iota((CHIPS, HALF), 0) * MOST
    member = ((column >= source) & (column < source + MOST)).astype(F32)
    row = jnp.sum(member * (column - source).astype(F32), axis=0, keepdims=True).astype(jnp.int32)
    spread = jnp.where(iota((128, HALF), 0) == row, best, 0.0)
    back = lax.dot_general(
        member, spread, (((1,), (1,)), ((), ())),
        precision=lax.Precision.HIGHEST, preferred_element_type=F32,
    )
    back_ref[...] = back.reshape(CHIPS, 1, 128)


def finish(back_ref, place_ref, out_ref):
    back = back_ref[...].reshape(CHIPS, 128)
    place = place_ref[...]
    first = iota((CHIPS, ROWS), 0)
    cluster_id = first // PLANES * USED + first % PLANES
    start = jnp.where(first % PLANES < USED, cluster_id * MOST, -MOST)
    member = ((place >= start) & (place < start + MOST)).astype(F32)
    rank = place - jnp.sum(member * start.astype(F32), axis=0, keepdims=True).astype(jnp.int32)
    columns = lax.dot_general(
        back, member, (((0,), (0,)), ((), ())),
        precision=lax.Precision.HIGHEST, preferred_element_type=F32,
    )
    out_ref[...] = jnp.sum(
        jnp.where(iota((128, ROWS), 0) == rank, columns, 0.0), axis=0, keepdims=True
    )


PARAMS = pltpu.CompilerParams(vmem_limit_bytes=24 * 1024 * 1024)


def per_device(embeddings, cluster_ids, order):
    shape = jax.ShapeDtypeStruct
    send, place = pl.pallas_call(
        prepare,
        out_shape=(shape((CHIPS, CHUNK, 128), BF16), shape((1, ROWS), jnp.int32)),
        compiler_params=PARAMS,
    )(embeddings, cluster_ids.reshape(1, ROWS), order.reshape(1, ROWS))
    got = lax.all_to_all(send, CHIP_AXES, split_axis=0, concat_axis=0, tiled=True)
    other = lax.ppermute(got, "c", [(0, 1), (1, 0)])
    cost = pl.CostEstimate(flops=2 * HALF * HALF * WIDTH, bytes_accessed=8 << 20, transcendentals=0)
    rows, query_late, best = pl.pallas_call(
        own_scores,
        out_shape=(shape((HALF, WIDTH), BF16), shape((1, HALF), F32), shape((8, HALF), F32)),
        scratch_shapes=[pltpu.VMEM((HALF, 1), F32)],
        compiler_params=PARAMS,
        cost_estimate=cost,
    )(got)
    back = pl.pallas_call(
        other_scores,
        out_shape=shape((CHIPS, 1, 128), F32),
        scratch_shapes=[pltpu.VMEM((HALF, WIDTH), BF16), pltpu.VMEM((HALF, 1), F32)],
        compiler_params=PARAMS,
        cost_estimate=cost,
    )(other, rows, query_late, best)
    returned = lax.all_to_all(back, CHIP_AXES, split_axis=0, concat_axis=0, tiled=True)
    nearest = pl.pallas_call(
        finish,
        out_shape=shape((1, ROWS), F32),
        compiler_params=PARAMS,
    )(returned, place)
    return nearest.reshape(ROWS)


def solution(mesh):
    fine = Mesh(mesh.devices.reshape(4, 4, PLANES, 2), AXES)
    return jax.shard_map(
        per_device,
        mesh=fine,
        in_specs=(P(AXES, None), P(AXES, None), P(AXES)),
        out_specs=P(AXES),
        check_vma=False,
    )
```

```python
import jax
import jax.numpy as jnp
from jax import lax
from jax.experimental import pallas as pl
from jax.experimental.pallas import tpu as pltpu
from jax.sharding import Mesh, PartitionSpec as P

CLUSTERS = 48
MOST = 24
WIDTH = 1024
ROWS = 384
CHIPS = 64
PLANES = 4
USED = 3
BLOCKS = WIDTH // 128
CHUNK = BLOCKS * MOST + 8
HALF = CHIPS * MOST
TILE = 16 * MOST
TOP = 65535
LOW = 64
PIECES = 3
PARTS = 4
F32 = jnp.float32
BF16 = jnp.bfloat16
AXES = ("x", "y", "z", "c")
CHIP_AXES = ("x", "y", "z")


def iota(shape, dim):
    return lax.broadcasted_iota(jnp.int32, shape, dim)


def chunk_of(cluster):
    return cluster // USED * PLANES + cluster % USED


def prepare(
    emb_hbm, cluster_hbm, order_hbm, send_hbm, place_ref,
    emb_ref, cluster_ref, order_ref, send_ref, sem, send_sem,
):
    copies = [
        pltpu.make_async_copy(cluster_hbm, cluster_ref, sem.at[PIECES]),
        pltpu.make_async_copy(order_hbm, order_ref, sem.at[PIECES + 1]),
    ]
    piece = ROWS // PIECES
    for one in range(PIECES):
        rows = pl.ds(one * piece, piece)
        copies.append(
            pltpu.make_async_copy(emb_hbm.at[rows, :], emb_ref.at[rows, :], sem.at[one])
        )
    for copy in copies:
        copy.start()
    copies[0].wait()
    copies[1].wait()
    cluster = cluster_ref[...]
    hot = (iota((CLUSTERS, ROWS), 0) == cluster).astype(BF16)
    before = (iota((ROWS, ROWS), 0) < iota((ROWS, ROWS), 1)).astype(BF16)
    counts = jnp.dot(hot, before, preferred_element_type=F32)
    rank = jnp.sum(counts * hot.astype(F32), axis=0, keepdims=True).astype(jnp.int32)
    slot = cluster * MOST + rank
    place_ref[...] = slot

    late = TOP - order_ref[...].reshape(1, ROWS)
    high = (late >> 8).astype(F32)
    low = (late & 255).astype(F32)
    lane = iota((128, ROWS), 0)
    coded = jnp.where(lane == rank, high, 0.0) + jnp.where(lane == rank + LOW, low, 0.0)
    orders = lax.dot_general(
        hot, coded.astype(BF16), (((1,), (1,)), ((), ())), preferred_element_type=F32
    )

    for unused in range(USED, CHIPS, PLANES):
        send_ref[unused] = jnp.zeros((CHUNK, 128), BF16)
    units = []
    for one in range(PIECES):
        copies[2 + one].wait()
        emb = emb_ref[one * piece : (one + 1) * piece, :]
        total = jnp.sum(emb * emb, axis=1, keepdims=True)
        units.append((emb * lax.rsqrt(total + 1e-06)).astype(BF16))
    unit = jnp.concatenate(units, axis=0)
    step = CLUSTERS // PARTS
    share = CHIPS // PARTS
    sends = []
    for part in range(PARTS):
        rows = step * MOST
        pick = (iota((rows, ROWS), 0) + part * rows == slot).astype(BF16)
        taken = jnp.dot(pick, unit, preferred_element_type=F32).astype(BF16)
        for one in range(step):
            cluster_id = part * step + one
            to = chunk_of(cluster_id)
            for block in range(BLOCKS):
                send_ref[to, block * MOST : (block + 1) * MOST, :] = taken[
                    one * MOST : (one + 1) * MOST, block * 128 : (block + 1) * 128
                ]
            send_ref[to, BLOCKS * MOST : CHUNK, :] = jnp.broadcast_to(
                orders[cluster_id : cluster_id + 1, :], (8, 128)
            ).astype(BF16)
        chunks = pl.ds(part * share, share)
        sends.append(
            pltpu.make_async_copy(send_ref.at[chunks], send_hbm.at[chunks], send_sem.at[part])
        )
        sends[part].start()
    for send in sends:
        send.wait()


def key_lateness(got_ref):
    tile = got_ref[:, BLOCKS * MOST : CHUNK, :].astype(F32)
    row = iota((1, 8, 128), 1)
    lane = iota((1, 8, 128), 2)
    parts = []
    for first in range(0, MOST, 8):
        weight = jnp.where(lane == row + first, 256.0, 0.0)
        weight = weight + jnp.where(lane == row + (first + LOW), 1.0, 0.0)
        parts.append(tile * weight)
    wide = jnp.concatenate(parts, axis=1).reshape(HALF, 128)
    return jnp.sum(wide, axis=1, keepdims=True)


def unpacked(got_ref, first):
    rows = TILE // MOST
    return jnp.concatenate(
        [
            got_ref[
                first * rows : (first + 1) * rows, block * MOST : (block + 1) * MOST, :
            ].reshape(TILE, 128)
            for block in range(BLOCKS)
        ],
        axis=1,
    )


def best_of(keys, key_late, queries, query_late):
    scores = lax.dot_general(
        keys, queries, (((1,), (1,)), ((), ())), preferred_element_type=F32
    )
    kept = jnp.where(key_late > query_late, scores, -1.0)
    return jnp.max(kept.reshape(TILE // 8, 8, HALF), axis=0)


def own_scores(got_ref, rows_ref, query_late_ref, best_ref, late_ref):
    for part in range(HALF // TILE):
        rows_ref[part * TILE : (part + 1) * TILE, :] = unpacked(got_ref, part)
    late_ref[...] = jnp.broadcast_to(key_lateness(got_ref), (HALF, 128))
    query_late = jnp.transpose(late_ref[...])[0:1, :]
    query_late_ref[...] = query_late
    best = jnp.full((8, HALF), -1.0, F32)
    for part in range(HALF // TILE):
        rows = slice(part * TILE, (part + 1) * TILE)
        found = best_of(rows_ref[rows, :], late_ref[rows, 0:1], rows_ref[...], query_late)
        best = jnp.maximum(best, found)
    best_ref[...] = best


def other_scores(got_ref, rows_ref, query_late_ref, best_ref, back_ref, late_ref):
    late_ref[...] = jnp.broadcast_to(key_lateness(got_ref), (HALF, 128))
    best = best_ref[...]
    for part in range(HALF // TILE):
        rows = slice(part * TILE, (part + 1) * TILE)
        found = best_of(
            unpacked(got_ref, part), late_ref[rows, 0:1], rows_ref[...], query_late_ref[...]
        )
        best = jnp.maximum(best, found)
    best = jnp.max(best, axis=0, keepdims=True)
    column = iota((CHIPS, HALF), 1)
    source = iota((CHIPS, HALF), 0) * MOST
    member = ((column >= source) & (column < source + MOST)).astype(F32)
    row = jnp.sum(member * (column - source).astype(F32), axis=0, keepdims=True).astype(jnp.int32)
    spread = jnp.where(iota((128, HALF), 0) == row, best, 0.0)
    back = lax.dot_general(
        member, spread, (((1,), (1,)), ((), ())),
        precision=lax.Precision.HIGHEST, preferred_element_type=F32,
    )
    back_ref[...] = back.reshape(CHIPS, 1, 128)


def finish(back_ref, place_ref, out_ref):
    back = back_ref[...].reshape(CHIPS, 128)
    place = place_ref[...]
    first = iota((CHIPS, ROWS), 0)
    cluster_id = first // PLANES * USED + first % PLANES
    start = jnp.where(first % PLANES < USED, cluster_id * MOST, -MOST)
    member = ((place >= start) & (place < start + MOST)).astype(F32)
    rank = place - jnp.sum(member * start.astype(F32), axis=0, keepdims=True).astype(jnp.int32)
    columns = lax.dot_general(
        back, member, (((0,), (0,)), ((), ())),
        precision=lax.Precision.HIGHEST, preferred_element_type=F32,
    )
    out_ref[...] = jnp.sum(
        jnp.where(iota((128, ROWS), 0) == rank, columns, 0.0), axis=0
    )


PARAMS = pltpu.CompilerParams(vmem_limit_bytes=24 * 1024 * 1024)


def per_device(embeddings, cluster_ids, order):
    shape = jax.ShapeDtypeStruct
    send, place = pl.pallas_call(
        prepare,
        out_shape=(shape((CHIPS, CHUNK, 128), BF16), shape((1, ROWS), jnp.int32)),
        in_specs=[pl.BlockSpec(memory_space=pltpu.HBM)] * 3,
        out_specs=(
            pl.BlockSpec(memory_space=pltpu.HBM),
            pl.BlockSpec(memory_space=pltpu.VMEM),
        ),
        scratch_shapes=[
            pltpu.VMEM((ROWS, WIDTH), F32),
            pltpu.VMEM((1, ROWS), jnp.int32),
            pltpu.VMEM((ROWS,), jnp.int32),
            pltpu.VMEM((CHIPS, CHUNK, 128), BF16),
            pltpu.SemaphoreType.DMA((PIECES + 2,)),
            pltpu.SemaphoreType.DMA((PARTS,)),
        ],
        compiler_params=pltpu.CompilerParams(vmem_limit_bytes=60 * 1024 * 1024),
    )(embeddings, cluster_ids.reshape(1, ROWS), order)
    got = lax.all_to_all(send, CHIP_AXES, split_axis=0, concat_axis=0, tiled=True)
    other = lax.ppermute(got, "c", [(0, 1), (1, 0)])
    cost = pl.CostEstimate(flops=2 * HALF * HALF * WIDTH, bytes_accessed=8 << 20, transcendentals=0)
    rows, query_late, best = pl.pallas_call(
        own_scores,
        out_shape=(shape((HALF, WIDTH), BF16), shape((1, HALF), F32), shape((8, HALF), F32)),
        scratch_shapes=[pltpu.VMEM((HALF, 128), F32)],
        compiler_params=PARAMS,
        cost_estimate=cost,
    )(got)
    back = pl.pallas_call(
        other_scores,
        out_shape=shape((CHIPS, 1, 128), F32),
        scratch_shapes=[pltpu.VMEM((HALF, 128), F32)],
        compiler_params=PARAMS,
        cost_estimate=cost,
    )(other, rows, query_late, best)
    returned = lax.all_to_all(back, CHIP_AXES, split_axis=0, concat_axis=0, tiled=True)
    return pl.pallas_call(
        finish,
        out_shape=shape((ROWS,), F32),
        compiler_params=PARAMS,
    )(returned, place)


def solution(mesh):
    fine = Mesh(mesh.devices.reshape(4, 4, PLANES, 2), AXES)
    return jax.shard_map(
        per_device,
        mesh=fine,
        in_specs=(P(AXES, None), P(AXES, None), P(AXES)),
        out_specs=P(AXES),
        check_vma=False,
    )
```

```python
import jax
import jax.numpy as jnp
from jax import lax
from jax.experimental import pallas as pl
from jax.experimental.pallas import tpu as pltpu
from jax.sharding import Mesh, PartitionSpec as P

CLUSTERS = 48
MOST = 24
WIDTH = 1024
ROWS = 384
CHIPS = 64
PLANES = 4
USED = 3
BLOCKS = WIDTH // 128
CHUNK = BLOCKS * MOST + 8
HALF = CHIPS * MOST
TILE = 16 * MOST
TOP = 65535
LOW = 64
PIECES = 3
PARTS = 8
THIRD = 32
F32 = jnp.float32
BF16 = jnp.bfloat16
AXES = ("x", "y", "z", "c")
CHIP_AXES = ("x", "y", "z")


def iota(shape, dim):
    return lax.broadcasted_iota(jnp.int32, shape, dim)


def chunk_of(cluster):
    return cluster // USED * PLANES + cluster % USED


def prepare(
    emb_hbm, cluster_hbm, order_hbm, send_hbm, place_ref,
    emb_ref, cluster_ref, order_ref, send_ref, sem, send_sem,
):
    copies = [
        pltpu.make_async_copy(cluster_hbm, cluster_ref, sem.at[PIECES]),
        pltpu.make_async_copy(order_hbm, order_ref, sem.at[PIECES + 1]),
    ]
    piece = ROWS // PIECES
    for one in range(PIECES):
        rows = pl.ds(one * piece, piece)
        copies.append(
            pltpu.make_async_copy(emb_hbm.at[rows, :], emb_ref.at[rows, :], sem.at[one])
        )
    for copy in copies:
        copy.start()
    copies[0].wait()
    copies[1].wait()
    cluster = cluster_ref[...]
    hot = (iota((CLUSTERS, ROWS), 0) == cluster).astype(BF16)
    before = (iota((ROWS, ROWS), 0) < iota((ROWS, ROWS), 1)).astype(BF16)
    counts = jnp.dot(hot, before, preferred_element_type=F32)
    rank = jnp.sum(counts * hot.astype(F32), axis=0, keepdims=True).astype(jnp.int32)
    slot = cluster * MOST + rank
    place_ref[0:1, :] = cluster + ((cluster * 171) >> 9)
    place_ref[1:2, :] = rank

    late = TOP - order_ref[...].reshape(1, ROWS)
    high = (late >> 8).astype(F32)
    low = (late & 255).astype(F32)
    lane = iota((128, ROWS), 0)
    coded = jnp.where(lane == rank, high, 0.0) + jnp.where(lane == rank + LOW, low, 0.0)
    orders = lax.dot_general(
        hot, coded.astype(BF16), (((1,), (1,)), ((), ())), preferred_element_type=F32
    )

    for unused in range(USED, CHIPS, PLANES):
        send_ref[unused] = jnp.zeros((CHUNK, 128), BF16)
    units = []
    for one in range(PIECES):
        copies[2 + one].wait()
        emb = emb_ref[one * piece : (one + 1) * piece, :]
        total = jnp.sum(emb * emb, axis=1, keepdims=True)
        units.append((emb * lax.rsqrt(total + 1e-06)).astype(BF16))
    unit = jnp.concatenate(units, axis=0)
    step = CLUSTERS // PARTS
    share = CHIPS // PARTS
    sends = []
    for part in range(PARTS):
        rows = step * MOST
        pick = (iota((rows, ROWS), 0) + part * rows == slot).astype(BF16)
        taken = jnp.dot(pick, unit, preferred_element_type=F32).astype(BF16)
        for one in range(step):
            cluster_id = part * step + one
            to = chunk_of(cluster_id)
            for block in range(BLOCKS):
                send_ref[to, block * MOST : (block + 1) * MOST, :] = taken[
                    one * MOST : (one + 1) * MOST, block * 128 : (block + 1) * 128
                ]
            send_ref[to, BLOCKS * MOST : CHUNK, :] = jnp.broadcast_to(
                orders[cluster_id : cluster_id + 1, :], (8, 128)
            ).astype(BF16)
        chunks = pl.ds(part * share, share)
        sends.append(
            pltpu.make_async_copy(send_ref.at[chunks], send_hbm.at[chunks], send_sem.at[part])
        )
        sends[part].start()
    for send in sends:
        send.wait()


def key_lateness(got_ref, first, count):
    tile = got_ref[first : first + count, BLOCKS * MOST : CHUNK, :].astype(F32)
    row = iota((1, 8, 128), 1)
    lane = iota((1, 8, 128), 2)
    parts = []
    for start in range(0, MOST, 8):
        weight = jnp.where(lane == row + start, 256.0, 0.0)
        weight = weight + jnp.where(lane == row + (start + LOW), 1.0, 0.0)
        parts.append(tile * weight)
    wide = jnp.concatenate(parts, axis=1).reshape(count * MOST, 128)
    return jnp.sum(wide, axis=1, keepdims=True)


def unpacked(got_ref, first):
    rows = TILE // MOST
    return jnp.concatenate(
        [
            got_ref[
                first * rows : (first + 1) * rows, block * MOST : (block + 1) * MOST, :
            ].reshape(TILE, 128)
            for block in range(BLOCKS)
        ],
        axis=1,
    )


def best_of(keys, key_late, queries, query_late):
    scores = lax.dot_general(
        keys, queries, (((1,), (1,)), ((), ())), preferred_element_type=F32
    )
    kept = jnp.where(key_late > query_late, scores, -1.0)
    return jnp.max(kept.reshape(TILE // 8, 8, HALF), axis=0)


def own_scores(got_ref, rows_ref, query_late_ref, best_ref, late_ref):
    for part in range(HALF // TILE):
        rows_ref[part * TILE : (part + 1) * TILE, :] = unpacked(got_ref, part)
    late_ref[...] = jnp.broadcast_to(key_lateness(got_ref, 0, CHIPS), (HALF, 128))
    query_late = jnp.transpose(late_ref[...])[0:1, :]
    query_late_ref[...] = query_late
    best = jnp.full((8, HALF), -1.0, F32)
    for part in range(HALF // TILE):
        rows = slice(part * TILE, (part + 1) * TILE)
        found = best_of(rows_ref[rows, :], late_ref[rows, 0:1], rows_ref[...], query_late)
        best = jnp.maximum(best, found)
    best_ref[...] = best


def exact_parts(row):
    high = row.astype(BF16)
    rest = row - high.astype(F32)
    middle = rest.astype(BF16)
    low = (rest - middle.astype(F32)).astype(BF16)
    return high, middle, low


def other_scores(got_ref, rows_ref, query_late_ref, best_ref, back_ref):
    column = iota((CHIPS, HALF), 1)
    source = iota((CHIPS, HALF), 0) * MOST
    member = (column >= source) & (column < source + MOST)
    row = jnp.sum(jnp.where(member, column - source, 0), axis=0, keepdims=True)
    here = iota((THIRD, HALF), 0) == row
    best = best_ref[...]
    sources = TILE // MOST
    for part in range(HALF // TILE):
        found = best_of(
            unpacked(got_ref, part),
            key_lateness(got_ref, part * sources, sources),
            rows_ref[...],
            query_late_ref[...],
        )
        best = jnp.maximum(best, found)
    best = jnp.max(best, axis=0, keepdims=True)
    spread = [jnp.where(here, one.astype(F32), 0.0) for one in exact_parts(best)]
    spread.append(jnp.zeros((THIRD, HALF), F32))
    back = lax.dot_general(
        member.astype(BF16),
        jnp.concatenate(spread, axis=0).astype(BF16),
        (((1,), (1,)), ((), ())),
        preferred_element_type=F32,
    )
    back_ref[...] = back.reshape(CHIPS, 1, 128)


def finish(back_ref, place_ref, out_ref):
    back = back_ref[...].reshape(CHIPS, 128).astype(BF16)
    member = (iota((CHIPS, ROWS), 0) == place_ref[0:1, :]).astype(BF16)
    columns = lax.dot_general(
        back, member, (((0,), (0,)), ((), ())), preferred_element_type=F32
    )
    rank = place_ref[1:2, :]
    row = iota((THIRD, ROWS), 0)
    high, middle, low = (columns[one * THIRD : (one + 1) * THIRD, :] for one in range(3))
    out_ref[...] = jnp.sum(jnp.where(row == rank, (low + middle) + high, 0.0), axis=0)


PARAMS = pltpu.CompilerParams(vmem_limit_bytes=24 * 1024 * 1024)


def per_device(embeddings, cluster_ids, order):
    shape = jax.ShapeDtypeStruct
    send, place = pl.pallas_call(
        prepare,
        out_shape=(shape((CHIPS, CHUNK, 128), BF16), shape((2, ROWS), jnp.int32)),
        in_specs=[pl.BlockSpec(memory_space=pltpu.HBM)] * 3,
        out_specs=(
            pl.BlockSpec(memory_space=pltpu.HBM),
            pl.BlockSpec(memory_space=pltpu.VMEM),
        ),
        scratch_shapes=[
            pltpu.VMEM((ROWS, WIDTH), F32),
            pltpu.VMEM((1, ROWS), jnp.int32),
            pltpu.VMEM((ROWS,), jnp.int32),
            pltpu.VMEM((CHIPS, CHUNK, 128), BF16),
            pltpu.SemaphoreType.DMA((PIECES + 2,)),
            pltpu.SemaphoreType.DMA((PARTS,)),
        ],
        compiler_params=pltpu.CompilerParams(vmem_limit_bytes=60 * 1024 * 1024),
    )(embeddings, cluster_ids.reshape(1, ROWS), order)
    got = lax.all_to_all(send, CHIP_AXES, split_axis=0, concat_axis=0, tiled=True)
    other = lax.ppermute(got, "c", [(0, 1), (1, 0)])
    cost = pl.CostEstimate(flops=2 * HALF * HALF * WIDTH, bytes_accessed=8 << 20, transcendentals=0)
    rows, query_late, best = pl.pallas_call(
        own_scores,
        out_shape=(shape((HALF, WIDTH), BF16), shape((1, HALF), F32), shape((8, HALF), F32)),
        scratch_shapes=[pltpu.VMEM((HALF, 128), F32)],
        compiler_params=PARAMS,
        cost_estimate=cost,
    )(got)
    back = pl.pallas_call(
        other_scores,
        out_shape=shape((CHIPS, 1, 128), F32),
        compiler_params=PARAMS,
        cost_estimate=cost,
    )(other, rows, query_late, best)
    returned = lax.all_to_all(back, CHIP_AXES, split_axis=0, concat_axis=0, tiled=True)
    return pl.pallas_call(
        finish,
        out_shape=shape((ROWS,), F32),
        compiler_params=PARAMS,
    )(returned, place)


def solution(mesh):
    fine = Mesh(mesh.devices.reshape(4, 4, PLANES, 2), AXES)
    return jax.shard_map(
        per_device,
        mesh=fine,
        in_specs=(P(AXES, None), P(AXES, None), P(AXES)),
        out_specs=P(AXES),
        check_vma=False,
    )
```

```python
import jax
import jax.numpy as jnp
from jax import lax
from jax.experimental import pallas as pl
from jax.experimental.pallas import tpu as pltpu
from jax.sharding import Mesh, PartitionSpec as P

CLUSTERS = 48
MOST = 24
WIDTH = 1024
ROWS = 384
CHIPS = 64
PLANES = 4
USED = 3
BLOCKS = WIDTH // 128
CHUNK = BLOCKS * MOST + 8
HALF = CHIPS * MOST
TILE = 16 * MOST
TOP = 65535
LOW = 64
PIECES = 3
PARTS = 8
THIRD = 32
F32 = jnp.float32
BF16 = jnp.bfloat16
AXES = ("x", "y", "z", "c")
CHIP_AXES = ("x", "y", "z")
BACK_AXES = ("c", "x", "y", "z")


def iota(shape, dim):
    return lax.broadcasted_iota(jnp.int32, shape, dim)


def prepare(
    emb_hbm, cluster_hbm, order_hbm, send_hbm, place_ref,
    emb_ref, cluster_ref, order_ref, send_ref, zero_ref, sem, send_sem,
):
    copies = [
        pltpu.make_async_copy(cluster_hbm, cluster_ref, sem.at[PIECES]),
        pltpu.make_async_copy(order_hbm, order_ref, sem.at[PIECES + 1]),
    ]
    piece = ROWS // PIECES
    for one in range(PIECES):
        rows = pl.ds(one * piece, piece)
        copies.append(
            pltpu.make_async_copy(emb_hbm.at[rows, :], emb_ref.at[rows, :], sem.at[one])
        )
    for copy in copies:
        copy.start()
    zero_ref[...] = jnp.zeros((CHIPS // PLANES, CHUNK, 128), BF16)
    zeros = pltpu.make_async_copy(zero_ref, send_hbm.at[:, USED], send_sem.at[PARTS])
    zeros.start()
    copies[0].wait()
    copies[1].wait()
    cluster = cluster_ref[...]
    hot = (iota((CLUSTERS, ROWS), 0) == cluster).astype(BF16)
    before = (iota((ROWS, ROWS), 0) < iota((ROWS, ROWS), 1)).astype(BF16)
    counts = jnp.dot(hot, before, preferred_element_type=F32)
    rank = jnp.sum(counts * hot.astype(F32), axis=0, keepdims=True).astype(jnp.int32)
    slot = cluster * MOST + rank
    place_ref[0:1, :] = cluster + ((cluster * 171) >> 9)
    place_ref[1:2, :] = rank

    late = TOP - order_ref[...].reshape(1, ROWS)
    high = (late >> 8).astype(F32)
    low = (late & 255).astype(F32)
    lane = iota((128, ROWS), 0)
    coded = jnp.where(lane == rank, high, 0.0) + jnp.where(lane == rank + LOW, low, 0.0)
    orders = lax.dot_general(
        hot, coded.astype(BF16), (((1,), (1,)), ((), ())), preferred_element_type=F32
    )

    units = []
    for one in range(PIECES):
        copies[2 + one].wait()
        emb = emb_ref[one * piece : (one + 1) * piece, :]
        total = jnp.sum(emb * emb, axis=1, keepdims=True)
        units.append((emb * lax.rsqrt(total + 1e-06)).astype(BF16))
    unit = jnp.concatenate(units, axis=0)
    step = CLUSTERS // PARTS
    share = step // USED
    sends = [zeros]
    for part in range(PARTS):
        rows = step * MOST
        pick = (iota((rows, ROWS), 0) + part * rows == slot).astype(BF16)
        taken = jnp.dot(pick, unit, preferred_element_type=F32).astype(BF16)
        for one in range(step):
            cluster_id = part * step + one
            to, plane = divmod(cluster_id, USED)
            for block in range(BLOCKS):
                send_ref[to, plane, block * MOST : (block + 1) * MOST, :] = taken[
                    one * MOST : (one + 1) * MOST, block * 128 : (block + 1) * 128
                ]
            send_ref[to, plane, BLOCKS * MOST : CHUNK, :] = jnp.broadcast_to(
                orders[cluster_id : cluster_id + 1, :], (8, 128)
            ).astype(BF16)
        chunks = pl.ds(part * share, share)
        send = pltpu.make_async_copy(
            send_ref.at[chunks], send_hbm.at[chunks, 0:USED], send_sem.at[part]
        )
        send.start()
        sends.append(send)
    for send in sends:
        send.wait()


def key_lateness(got_ref, first, count):
    tile = got_ref[first : first + count, BLOCKS * MOST : CHUNK, :].astype(F32)
    row = iota((1, 8, 128), 1)
    lane = iota((1, 8, 128), 2)
    parts = []
    for start in range(0, MOST, 8):
        weight = jnp.where(lane == row + start, 256.0, 0.0)
        weight = weight + jnp.where(lane == row + (start + LOW), 1.0, 0.0)
        parts.append(tile * weight)
    wide = jnp.concatenate(parts, axis=1).reshape(count * MOST, 128)
    return jnp.sum(wide, axis=1, keepdims=True)


def unpacked(got_ref, first):
    rows = TILE // MOST
    return jnp.concatenate(
        [
            got_ref[
                first * rows : (first + 1) * rows, block * MOST : (block + 1) * MOST, :
            ].reshape(TILE, 128)
            for block in range(BLOCKS)
        ],
        axis=1,
    )


def fold(scores):
    rows, columns = scores.shape
    return jnp.max(scores.reshape(rows // 8, 8, columns), axis=0)


def score(keys, queries):
    return lax.dot_general(
        keys, queries, (((1,), (1,)), ((), ())), preferred_element_type=F32
    )


def own_scores(got_ref, rows_ref, query_late_ref, best_ref, late_ref):
    for part in range(HALF // TILE):
        rows_ref[part * TILE : (part + 1) * TILE, :] = unpacked(got_ref, part)
    late_ref[...] = jnp.broadcast_to(key_lateness(got_ref, 0, CHIPS), (HALF, 128))
    query_late = jnp.transpose(late_ref[...])[0:1, :]
    query_late_ref[...] = query_late
    best = jnp.full((8, HALF), -1.0, F32)
    for part in range(HALF // TILE):
        rows = slice(part * TILE, (part + 1) * TILE)
        scores = score(rows_ref[rows, :], rows_ref[...])
        kept = jnp.where(late_ref[rows, 0:1] > query_late, scores, -1.0)
        best = jnp.maximum(best, fold(kept))
    best_ref[...] = best


def exact_parts(values):
    high = values.astype(BF16)
    rest = values - high.astype(F32)
    middle = rest.astype(BF16)
    low = (rest - middle.astype(F32)).astype(BF16)
    return high, middle, low


def by_source(best):
    column = iota((CHIPS, HALF), 1)
    source = iota((CHIPS, HALF), 0) * MOST
    member = (column >= source) & (column < source + MOST)
    row = jnp.sum(jnp.where(member, column - source, 0), axis=0, keepdims=True)
    here = iota((THIRD, HALF), 0) == row
    spread = [jnp.where(here, one.astype(F32), 0.0) for one in exact_parts(best)]
    spread.append(jnp.zeros((THIRD, HALF), F32))
    parts = lax.dot_general(
        member.astype(BF16),
        jnp.concatenate(spread, axis=0).astype(BF16),
        (((1,), (1,)), ((), ())),
        preferred_element_type=F32,
    )
    return (pltpu.roll(parts, 2 * THIRD, 1) + pltpu.roll(parts, 3 * THIRD, 1)) + parts


def cross(got_ref, rows_ref, query_late_ref, best_ref, back_ref, first, queries, own_at, other_at):
    sources = TILE // MOST
    best = best_ref[:, 0:queries]
    query_late = query_late_ref[:, 0:queries]
    if first:
        back_ref[other_at : other_at + first] = jnp.full((first, 1, 128), -1.0, F32)
    for source in range(first, CHIPS, sources):
        scores = score(unpacked(got_ref, source // sources), rows_ref[0:queries, :])
        later = key_lateness(got_ref, source, sources) > query_late
        best = jnp.maximum(best, fold(jnp.where(later, scores, -1.0)))
        turned = jnp.where(later, -1.0, scores)
        wide = turned[:, 0:128]
        for start in range(128, queries, 128):
            wide = jnp.maximum(wide, turned[:, start : start + 128])
        found = jnp.max(wide, axis=1, keepdims=True)
        found = jnp.broadcast_to(found, (TILE, 128)).reshape(sources, MOST, 128)
        shape = (sources, MOST, 128)
        placed = jnp.where(iota(shape, 1) == iota(shape, 2), found, 0.0)
        back_ref[other_at + source : other_at + source + sources] = jnp.sum(
            placed, axis=1
        ).reshape(sources, 1, 128)
    if queries < HALF:
        best = jnp.concatenate([best, best_ref[:, queries:HALF]], axis=1)
    best = jnp.max(best, axis=0, keepdims=True)
    back_ref[own_at : own_at + CHIPS] = by_source(best).reshape(CHIPS, 1, 128)


def other_scores(got_ref, rows_ref, query_late_ref, best_ref, back_ref):
    core = lax.axis_index("c")
    refs = (got_ref, rows_ref, query_late_ref, best_ref, back_ref)

    @pl.when(core == 0)
    def _():
        cross(*refs, first=0, queries=HALF // 2, own_at=0, other_at=CHIPS)

    @pl.when(core == 1)
    def _():
        cross(*refs, first=CHIPS // 2, queries=HALF, own_at=CHIPS, other_at=0)


def finish(back_ref, place_ref, out_ref):
    back = jnp.maximum(back_ref[0:CHIPS], back_ref[CHIPS : 2 * CHIPS]).reshape(CHIPS, 128)
    member = (iota((CHIPS, ROWS), 0) == place_ref[0:1, :]).astype(BF16)
    columns = lax.dot_general(
        jnp.concatenate(exact_parts(back), axis=0),
        jnp.concatenate([member, member, member], axis=0),
        (((0,), (0,)), ((), ())),
        preferred_element_type=F32,
    )
    here = iota((THIRD, ROWS), 0) == place_ref[1:2, :]
    out_ref[...] = jnp.sum(jnp.where(here, columns[0:THIRD, :], 0.0), axis=0)


PARAMS = pltpu.CompilerParams(vmem_limit_bytes=24 * 1024 * 1024)


def per_device(embeddings, cluster_ids, order):
    shape = jax.ShapeDtypeStruct
    send, place = pl.pallas_call(
        prepare,
        out_shape=(shape((CHIPS // PLANES, PLANES, CHUNK, 128), BF16), shape((2, ROWS), jnp.int32)),
        in_specs=[pl.BlockSpec(memory_space=pltpu.HBM)] * 3,
        out_specs=(
            pl.BlockSpec(memory_space=pltpu.HBM),
            pl.BlockSpec(memory_space=pltpu.VMEM),
        ),
        scratch_shapes=[
            pltpu.VMEM((ROWS, WIDTH), F32),
            pltpu.VMEM((1, ROWS), jnp.int32),
            pltpu.VMEM((ROWS,), jnp.int32),
            pltpu.VMEM((CHIPS // PLANES, USED, CHUNK, 128), BF16),
            pltpu.VMEM((CHIPS // PLANES, CHUNK, 128), BF16),
            pltpu.SemaphoreType.DMA((PIECES + 2,)),
            pltpu.SemaphoreType.DMA((PARTS + 1,)),
        ],
        compiler_params=pltpu.CompilerParams(vmem_limit_bytes=60 * 1024 * 1024),
    )(embeddings, cluster_ids.reshape(1, ROWS), order)
    send = send.reshape(CHIPS, CHUNK, 128)
    got = lax.all_to_all(send, CHIP_AXES, split_axis=0, concat_axis=0, tiled=True)
    other = lax.ppermute(got, "c", [(0, 1), (1, 0)])
    cost = pl.CostEstimate(flops=2 * HALF * HALF * WIDTH, bytes_accessed=8 << 20, transcendentals=0)
    rows, query_late, best = pl.pallas_call(
        own_scores,
        out_shape=(shape((HALF, WIDTH), BF16), shape((1, HALF), F32), shape((8, HALF), F32)),
        scratch_shapes=[pltpu.VMEM((HALF, 128), F32)],
        compiler_params=PARAMS,
        cost_estimate=cost,
    )(got)
    back = pl.pallas_call(
        other_scores,
        out_shape=shape((2 * CHIPS, 1, 128), F32),
        compiler_params=PARAMS,
        cost_estimate=cost,
    )(other, rows, query_late, best)
    returned = lax.all_to_all(back, BACK_AXES, split_axis=0, concat_axis=0, tiled=True)
    return pl.pallas_call(
        finish,
        out_shape=shape((ROWS,), F32),
        compiler_params=PARAMS,
    )(returned, place)


def solution(mesh):
    fine = Mesh(mesh.devices.reshape(4, 4, PLANES, 2), AXES)
    return jax.shard_map(
        per_device,
        mesh=fine,
        in_specs=(P(AXES, None), P(AXES, None), P(AXES)),
        out_specs=P(AXES),
        check_vma=False,
    )
```

```python
import jax
import jax.numpy as jnp
from jax import lax
from jax.experimental import pallas as pl
from jax.experimental.pallas import tpu as pltpu
from jax.sharding import Mesh, PartitionSpec as P

CLUSTERS = 48
MOST = 24
WIDTH = 1024
ROWS = 384
CHIPS = 64
PLANES = 4
USED = 3
BLOCKS = WIDTH // 128
CHUNK = BLOCKS * MOST + 8
HALF = CHIPS * MOST
TILE = 16 * MOST
TOP = 65535
LOW = 64
PIECES = 3
PARTS = 8
THIRD = 32
F32 = jnp.float32
BF16 = jnp.bfloat16
AXES = ("x", "y", "z", "c")
CHIP_AXES = ("x", "y", "z")
BACK_AXES = ("c", "x", "y", "z")


def iota(shape, dim):
    return lax.broadcasted_iota(jnp.int32, shape, dim)


def chunk_of(cluster):
    return cluster // USED * PLANES + cluster % USED


def prepare(
    emb_hbm, cluster_hbm, order_hbm, send_hbm, place_ref,
    emb_ref, cluster_ref, order_ref, send_ref, sem, send_sem,
):
    copies = [
        pltpu.make_async_copy(cluster_hbm, cluster_ref, sem.at[PIECES]),
        pltpu.make_async_copy(order_hbm, order_ref, sem.at[PIECES + 1]),
    ]
    piece = ROWS // PIECES
    for one in range(PIECES):
        rows = pl.ds(one * piece, piece)
        copies.append(
            pltpu.make_async_copy(emb_hbm.at[rows, :], emb_ref.at[rows, :], sem.at[one])
        )
    for copy in copies:
        copy.start()
    copies[0].wait()
    copies[1].wait()
    cluster = cluster_ref[...]
    hot = (iota((CLUSTERS, ROWS), 0) == cluster).astype(BF16)
    before = (iota((ROWS, ROWS), 0) < iota((ROWS, ROWS), 1)).astype(BF16)
    counts = jnp.dot(hot, before, preferred_element_type=F32)
    rank = jnp.sum(counts * hot.astype(F32), axis=0, keepdims=True).astype(jnp.int32)
    slot = cluster * MOST + rank
    place_ref[0:1, :] = cluster + ((cluster * 171) >> 9)
    place_ref[1:2, :] = rank

    late = TOP - order_ref[...].reshape(1, ROWS)
    high = (late >> 8).astype(F32)
    low = (late & 255).astype(F32)
    lane = iota((128, ROWS), 0)
    coded = jnp.where(lane == rank, high, 0.0) + jnp.where(lane == rank + LOW, low, 0.0)
    orders = lax.dot_general(
        hot, coded.astype(BF16), (((1,), (1,)), ((), ())), preferred_element_type=F32
    )

    for unused in range(USED, CHIPS, PLANES):
        send_ref[unused] = jnp.zeros((CHUNK, 128), BF16)
    units = []
    for one in range(PIECES):
        copies[2 + one].wait()
        emb = emb_ref[one * piece : (one + 1) * piece, :]
        total = jnp.sum(emb * emb, axis=1, keepdims=True)
        units.append((emb * lax.rsqrt(total + 1e-06)).astype(BF16))
    unit = jnp.concatenate(units, axis=0)
    step = CLUSTERS // PARTS
    share = CHIPS // PARTS
    sends = []
    for part in range(PARTS):
        rows = step * MOST
        pick = (iota((rows, ROWS), 0) + part * rows == slot).astype(BF16)
        taken = jnp.dot(pick, unit, preferred_element_type=F32).astype(BF16)
        for one in range(step):
            cluster_id = part * step + one
            to = chunk_of(cluster_id)
            for block in range(BLOCKS):
                send_ref[to, block * MOST : (block + 1) * MOST, :] = taken[
                    one * MOST : (one + 1) * MOST, block * 128 : (block + 1) * 128
                ]
            send_ref[to, BLOCKS * MOST : CHUNK, :] = jnp.broadcast_to(
                orders[cluster_id : cluster_id + 1, :], (8, 128)
            ).astype(BF16)
        chunks = pl.ds(part * share, share)
        sends.append(
            pltpu.make_async_copy(send_ref.at[chunks], send_hbm.at[chunks], send_sem.at[part])
        )
        sends[part].start()
    for send in sends:
        send.wait()


def key_lateness(got_ref, first, count):
    tile = got_ref[first : first + count, BLOCKS * MOST : CHUNK, :].astype(F32)
    row = iota((1, 8, 128), 1)
    lane = iota((1, 8, 128), 2)
    parts = []
    for start in range(0, MOST, 8):
        weight = jnp.where(lane == row + start, 256.0, 0.0)
        weight = weight + jnp.where(lane == row + (start + LOW), 1.0, 0.0)
        parts.append(tile * weight)
    wide = jnp.concatenate(parts, axis=1).reshape(count * MOST, 128)
    return jnp.sum(wide, axis=1, keepdims=True)


def unpacked(got_ref, first):
    rows = TILE // MOST
    return jnp.concatenate(
        [
            got_ref[
                first * rows : (first + 1) * rows, block * MOST : (block + 1) * MOST, :
            ].reshape(TILE, 128)
            for block in range(BLOCKS)
        ],
        axis=1,
    )


def fold(scores):
    rows, columns = scores.shape
    return jnp.max(scores.reshape(rows // 8, 8, columns), axis=0)


def score(keys, queries):
    return lax.dot_general(
        keys, queries, (((1,), (1,)), ((), ())), preferred_element_type=F32
    )


def own_scores(got_ref, rows_ref, query_late_ref, best_ref, late_ref):
    for part in range(HALF // TILE):
        rows_ref[part * TILE : (part + 1) * TILE, :] = unpacked(got_ref, part)
    late_ref[...] = jnp.broadcast_to(key_lateness(got_ref, 0, CHIPS), (HALF, 128))
    query_late = jnp.transpose(late_ref[...])[0:1, :]
    query_late_ref[...] = query_late
    best = jnp.full((8, HALF), -1.0, F32)
    for part in range(HALF // TILE):
        rows = slice(part * TILE, (part + 1) * TILE)
        scores = score(rows_ref[rows, :], rows_ref[...])
        kept = jnp.where(late_ref[rows, 0:1] > query_late, scores, -1.0)
        best = jnp.maximum(best, fold(kept))
    best_ref[...] = best


def exact_parts(values):
    high = values.astype(BF16)
    rest = values - high.astype(F32)
    middle = rest.astype(BF16)
    low = (rest - middle.astype(F32)).astype(BF16)
    return high, middle, low


def by_source(best):
    sources = TILE // MOST
    column = iota((sources, TILE), 1)
    source = iota((sources, TILE), 0) * MOST
    member = (column >= source) & (column < source + MOST)
    row = jnp.sum(jnp.where(member, column - source, 0), axis=0, keepdims=True)
    here = iota((THIRD, TILE), 0) == row
    member = member.astype(F32).astype(BF16)
    none = jnp.zeros((THIRD, TILE), F32)
    groups = []
    for start in range(0, HALF, TILE):
        values = exact_parts(best[:, start : start + TILE])
        spread = [jnp.where(here, one.astype(F32), 0.0) for one in values]
        parts = lax.dot_general(
            member,
            jnp.concatenate(spread + [none], axis=0).astype(BF16),
            (((1,), (1,)), ((), ())),
            preferred_element_type=F32,
        )
        groups.append(
            (pltpu.roll(parts, 2 * THIRD, 1) + pltpu.roll(parts, 3 * THIRD, 1)) + parts
        )
    return jnp.concatenate(groups, axis=0)


def cross(got_ref, rows_ref, query_late_ref, best_ref, back_ref, first, queries, own_at, other_at):
    sources = TILE // MOST
    best = best_ref[:, 0:queries]
    query_late = query_late_ref[:, 0:queries]
    if first:
        back_ref[other_at : other_at + first] = jnp.full((first, 1, 128), -1.0, F32)
    for source in range(first, CHIPS, sources):
        scores = score(unpacked(got_ref, source // sources), rows_ref[0:queries, :])
        later = key_lateness(got_ref, source, sources) > query_late
        best = jnp.maximum(best, fold(jnp.where(later, scores, -1.0)))
        turned = jnp.where(later, -1.0, scores)
        wide = turned[:, 0:128]
        for start in range(128, queries, 128):
            wide = jnp.maximum(wide, turned[:, start : start + 128])
        found = jnp.max(wide, axis=1, keepdims=True)
        found = jnp.broadcast_to(found, (TILE, 128)).reshape(sources, MOST, 128)
        shape = (sources, MOST, 128)
        placed = jnp.where(iota(shape, 1) == iota(shape, 2), found, 0.0)
        back_ref[other_at + source : other_at + source + sources] = jnp.sum(
            placed, axis=1
        ).reshape(sources, 1, 128)
    if queries < HALF:
        best = jnp.concatenate([best, best_ref[:, queries:HALF]], axis=1)
    best = jnp.max(best, axis=0, keepdims=True)
    back_ref[own_at : own_at + CHIPS] = by_source(best).reshape(CHIPS, 1, 128)


def other_scores(got_ref, rows_ref, query_late_ref, best_ref, back_ref):
    core = lax.axis_index("c")
    refs = (got_ref, rows_ref, query_late_ref, best_ref, back_ref)

    @pl.when(core == 0)
    def _():
        cross(*refs, first=0, queries=HALF // 2, own_at=0, other_at=CHIPS)

    @pl.when(core == 1)
    def _():
        cross(*refs, first=CHIPS // 2, queries=HALF, own_at=CHIPS, other_at=0)


def finish(back_ref, place_ref, out_ref):
    back = jnp.maximum(back_ref[0:CHIPS], back_ref[CHIPS : 2 * CHIPS]).reshape(CHIPS, 128)
    member = (iota((CHIPS, ROWS), 0) == place_ref[0:1, :]).astype(BF16)
    columns = lax.dot_general(
        jnp.concatenate(exact_parts(back), axis=0),
        jnp.concatenate([member, member, member], axis=0),
        (((0,), (0,)), ((), ())),
        preferred_element_type=F32,
    )
    here = iota((THIRD, ROWS), 0) == place_ref[1:2, :]
    out_ref[...] = jnp.sum(jnp.where(here, columns[0:THIRD, :], 0.0), axis=0)


PARAMS = pltpu.CompilerParams(vmem_limit_bytes=24 * 1024 * 1024)


def per_device(embeddings, cluster_ids, order):
    shape = jax.ShapeDtypeStruct
    send, place = pl.pallas_call(
        prepare,
        out_shape=(shape((CHIPS, CHUNK, 128), BF16), shape((2, ROWS), jnp.int32)),
        in_specs=[pl.BlockSpec(memory_space=pltpu.HBM)] * 3,
        out_specs=(
            pl.BlockSpec(memory_space=pltpu.HBM),
            pl.BlockSpec(memory_space=pltpu.VMEM),
        ),
        scratch_shapes=[
            pltpu.VMEM((ROWS, WIDTH), F32),
            pltpu.VMEM((1, ROWS), jnp.int32),
            pltpu.VMEM((ROWS,), jnp.int32),
            pltpu.VMEM((CHIPS, CHUNK, 128), BF16),
            pltpu.SemaphoreType.DMA((PIECES + 2,)),
            pltpu.SemaphoreType.DMA((PARTS,)),
        ],
        compiler_params=pltpu.CompilerParams(vmem_limit_bytes=60 * 1024 * 1024),
    )(embeddings, cluster_ids.reshape(1, ROWS), order)
    got = lax.all_to_all(send, CHIP_AXES, split_axis=0, concat_axis=0, tiled=True)
    other = lax.ppermute(got, "c", [(0, 1), (1, 0)])
    cost = pl.CostEstimate(flops=2 * HALF * HALF * WIDTH, bytes_accessed=8 << 20, transcendentals=0)
    rows, query_late, best = pl.pallas_call(
        own_scores,
        out_shape=(shape((HALF, WIDTH), BF16), shape((1, HALF), F32), shape((8, HALF), F32)),
        scratch_shapes=[pltpu.VMEM((HALF, 128), F32)],
        compiler_params=PARAMS,
        cost_estimate=cost,
    )(got)
    back = pl.pallas_call(
        other_scores,
        out_shape=shape((2 * CHIPS, 1, 128), F32),
        compiler_params=PARAMS,
        cost_estimate=cost,
    )(other, rows, query_late, best)
    returned = lax.all_to_all(back, BACK_AXES, split_axis=0, concat_axis=0, tiled=True)
    return pl.pallas_call(
        finish,
        out_shape=shape((ROWS,), F32),
        compiler_params=PARAMS,
    )(returned, place)


def solution(mesh):
    fine = Mesh(mesh.devices.reshape(4, 4, PLANES, 2), AXES)
    return jax.shard_map(
        per_device,
        mesh=fine,
        in_specs=(P(AXES, None), P(AXES, None), P(AXES)),
        out_specs=P(AXES),
        check_vma=False,
    )
```

```python
import jax
import jax.numpy as jnp
from jax import lax
from jax.experimental import pallas as pl
from jax.experimental.pallas import tpu as pltpu
from jax.sharding import Mesh, PartitionSpec as P

CLUSTERS = 48
MOST = 24
WIDTH = 1024
ROWS = 384
CHIPS = 64
PLANES = 4
USED = 3
BLOCKS = WIDTH // 128
CHUNK = BLOCKS * MOST + 8
HALF = CHIPS * MOST
TILE = 16 * MOST
TOP = 65535
LOW = 64
PIECES = 3
PARTS = 3
THIRD = 32
F32 = jnp.float32
BF16 = jnp.bfloat16
AXES = ("x", "y", "z", "c")
CHIP_AXES = ("x", "y", "z")
BACK_AXES = ("c", "x", "y", "z")


def iota(shape, dim):
    return lax.broadcasted_iota(jnp.int32, shape, dim)


def chunk_of(cluster):
    return cluster // USED * PLANES + cluster % USED


def prepare(
    emb_hbm, cluster_hbm, order_hbm, send_ref, place_ref,
    emb_ref, cluster_ref, order_ref, sem,
):
    copies = [
        pltpu.make_async_copy(cluster_hbm, cluster_ref, sem.at[PIECES]),
        pltpu.make_async_copy(order_hbm, order_ref, sem.at[PIECES + 1]),
    ]
    piece = ROWS // PIECES
    for one in range(PIECES):
        rows = pl.ds(one * piece, piece)
        copies.append(
            pltpu.make_async_copy(emb_hbm.at[rows, :], emb_ref.at[rows, :], sem.at[one])
        )
    for copy in copies:
        copy.start()
    copies[0].wait()
    copies[1].wait()
    cluster = cluster_ref[...]
    hot = (iota((CLUSTERS, ROWS), 0) == cluster).astype(BF16)
    before = (iota((ROWS, ROWS), 0) < iota((ROWS, ROWS), 1)).astype(BF16)
    counts = jnp.dot(hot, before, preferred_element_type=F32)
    rank = jnp.sum(counts * hot.astype(F32), axis=0, keepdims=True).astype(jnp.int32)
    slot = cluster * MOST + rank
    place_ref[0:1, :] = cluster + ((cluster * 171) >> 9)
    place_ref[1:2, :] = rank

    late = TOP - order_ref[...].reshape(1, ROWS)
    high = (late >> 8).astype(F32)
    low = (late & 255).astype(F32)
    lane = iota((128, ROWS), 0)
    coded = jnp.where(lane == rank, high, 0.0) + jnp.where(lane == rank + LOW, low, 0.0)
    orders = lax.dot_general(
        hot, coded.astype(BF16), (((1,), (1,)), ((), ())), preferred_element_type=F32
    )

    for unused in range(USED, CHIPS, PLANES):
        send_ref[unused] = jnp.zeros((CHUNK, 128), BF16)
    for unused in range(USED, CHIPS, PLANES):
        send_ref[unused] = jnp.zeros((CHUNK, 128), BF16)
    units = []
    for one in range(PIECES):
        copies[2 + one].wait()
        emb = emb_ref[one * piece : (one + 1) * piece, :]
        total = jnp.sum(emb * emb, axis=1, keepdims=True)
        units.append((emb * lax.rsqrt(total + 1e-06)).astype(BF16))
    unit = jnp.concatenate(units, axis=0)
    step = CLUSTERS // PARTS
    for part in range(PARTS):
        rows = step * MOST
        pick = (iota((rows, ROWS), 0) + part * rows == slot).astype(BF16)
        taken = jnp.dot(pick, unit, preferred_element_type=F32).astype(BF16)
        for one in range(step):
            cluster_id = part * step + one
            to = chunk_of(cluster_id)
            for block in range(BLOCKS):
                send_ref[to, block * MOST : (block + 1) * MOST, :] = taken[
                    one * MOST : (one + 1) * MOST, block * 128 : (block + 1) * 128
                ]
            send_ref[to, BLOCKS * MOST : CHUNK, :] = jnp.broadcast_to(
                orders[cluster_id : cluster_id + 1, :], (8, 128)
            ).astype(BF16)


def key_lateness(got_ref, first, count):
    tile = got_ref[first : first + count, BLOCKS * MOST : CHUNK, :].astype(F32)
    row = iota((1, 8, 128), 1)
    lane = iota((1, 8, 128), 2)
    parts = []
    for start in range(0, MOST, 8):
        weight = jnp.where(lane == row + start, 256.0, 0.0)
        weight = weight + jnp.where(lane == row + (start + LOW), 1.0, 0.0)
        parts.append(tile * weight)
    wide = jnp.concatenate(parts, axis=1).reshape(count * MOST, 128)
    return jnp.sum(wide, axis=1, keepdims=True)


def unpacked(got_ref, first):
    rows = TILE // MOST
    return jnp.concatenate(
        [
            got_ref[
                first * rows : (first + 1) * rows, block * MOST : (block + 1) * MOST, :
            ].reshape(TILE, 128)
            for block in range(BLOCKS)
        ],
        axis=1,
    )


def fold(scores):
    rows, columns = scores.shape
    return jnp.max(scores.reshape(rows // 8, 8, columns), axis=0)


def score(keys, queries):
    return lax.dot_general(
        keys, queries, (((1,), (1,)), ((), ())), preferred_element_type=F32
    )


def own_scores(got_ref, rows_ref, query_late_ref, best_ref, late_ref):
    for part in range(HALF // TILE):
        rows_ref[part * TILE : (part + 1) * TILE, :] = unpacked(got_ref, part)
    late_ref[...] = jnp.broadcast_to(key_lateness(got_ref, 0, CHIPS), (HALF, 128))
    query_late = jnp.transpose(late_ref[...])[0:1, :]
    query_late_ref[...] = query_late
    best = jnp.full((8, HALF), -1.0, F32)
    for part in range(HALF // TILE):
        rows = slice(part * TILE, (part + 1) * TILE)
        scores = score(rows_ref[rows, :], rows_ref[...])
        kept = jnp.where(late_ref[rows, 0:1] > query_late, scores, -1.0)
        best = jnp.maximum(best, fold(kept))
    best_ref[...] = best


def exact_parts(values):
    high = values.astype(BF16)
    rest = values - high.astype(F32)
    middle = rest.astype(BF16)
    low = (rest - middle.astype(F32)).astype(BF16)
    return high, middle, low


def by_source(best):
    sources = TILE // MOST
    column = iota((sources, TILE), 1)
    source = iota((sources, TILE), 0) * MOST
    member = (column >= source) & (column < source + MOST)
    row = jnp.sum(jnp.where(member, column - source, 0), axis=0, keepdims=True)
    here = iota((THIRD, TILE), 0) == row
    member = member.astype(F32).astype(BF16)
    none = jnp.zeros((THIRD, TILE), F32)
    groups = []
    for start in range(0, HALF, TILE):
        values = exact_parts(best[:, start : start + TILE])
        spread = [jnp.where(here, one.astype(F32), 0.0) for one in values]
        parts = lax.dot_general(
            member,
            jnp.concatenate(spread + [none], axis=0).astype(BF16),
            (((1,), (1,)), ((), ())),
            preferred_element_type=F32,
        )
        groups.append(
            (pltpu.roll(parts, 2 * THIRD, 1) + pltpu.roll(parts, 3 * THIRD, 1)) + parts
        )
    return jnp.concatenate(groups, axis=0)


def cross(got_ref, rows_ref, query_late_ref, best_ref, back_ref, first, queries, own_at, other_at):
    sources = TILE // MOST
    best = best_ref[:, 0:queries]
    query_late = query_late_ref[:, 0:queries]
    if first:
        back_ref[other_at : other_at + first] = jnp.full((first, 1, 128), -1.0, F32)
    for source in range(first, CHIPS, sources):
        scores = score(unpacked(got_ref, source // sources), rows_ref[0:queries, :])
        later = key_lateness(got_ref, source, sources) > query_late
        best = jnp.maximum(best, fold(jnp.where(later, scores, -1.0)))
        turned = jnp.where(later, -1.0, scores)
        wide = turned[:, 0:128]
        for start in range(128, queries, 128):
            wide = jnp.maximum(wide, turned[:, start : start + 128])
        found = jnp.max(wide, axis=1, keepdims=True)
        found = jnp.broadcast_to(found, (TILE, 128)).reshape(sources, MOST, 128)
        shape = (sources, MOST, 128)
        placed = jnp.where(iota(shape, 1) == iota(shape, 2), found, 0.0)
        back_ref[other_at + source : other_at + source + sources] = jnp.sum(
            placed, axis=1
        ).reshape(sources, 1, 128)
    if queries < HALF:
        best = jnp.concatenate([best, best_ref[:, queries:HALF]], axis=1)
    best = jnp.max(best, axis=0, keepdims=True)
    back_ref[own_at : own_at + CHIPS] = by_source(best).reshape(CHIPS, 1, 128)


def other_scores(got_ref, rows_ref, query_late_ref, best_ref, back_ref):
    core = lax.axis_index("c")
    refs = (got_ref, rows_ref, query_late_ref, best_ref, back_ref)

    @pl.when(core == 0)
    def _():
        cross(*refs, first=0, queries=HALF // 2, own_at=0, other_at=CHIPS)

    @pl.when(core == 1)
    def _():
        cross(*refs, first=CHIPS // 2, queries=HALF, own_at=CHIPS, other_at=0)


def finish(back_ref, place_ref, out_ref):
    back = jnp.maximum(back_ref[0:CHIPS], back_ref[CHIPS : 2 * CHIPS]).reshape(CHIPS, 128)
    member = (iota((CHIPS, ROWS), 0) == place_ref[0:1, :]).astype(BF16)
    columns = lax.dot_general(
        jnp.concatenate(exact_parts(back), axis=0),
        jnp.concatenate([member, member, member], axis=0),
        (((0,), (0,)), ((), ())),
        preferred_element_type=F32,
    )
    here = iota((THIRD, ROWS), 0) == place_ref[1:2, :]
    out_ref[...] = jnp.sum(jnp.where(here, columns[0:THIRD, :], 0.0), axis=0)


PARAMS = pltpu.CompilerParams(vmem_limit_bytes=24 * 1024 * 1024)


def per_device(embeddings, cluster_ids, order):
    shape = jax.ShapeDtypeStruct
    send, place = pl.pallas_call(
        prepare,
        out_shape=(shape((CHIPS, CHUNK, 128), BF16), shape((2, ROWS), jnp.int32)),
        in_specs=[pl.BlockSpec(memory_space=pltpu.HBM)] * 3,
        scratch_shapes=[
            pltpu.VMEM((ROWS, WIDTH), F32),
            pltpu.VMEM((1, ROWS), jnp.int32),
            pltpu.VMEM((ROWS,), jnp.int32),
            pltpu.SemaphoreType.DMA((PIECES + 2,)),
        ],
        compiler_params=pltpu.CompilerParams(vmem_limit_bytes=24 * 1024 * 1024),
    )(
        pltpu.with_memory_space_constraint(embeddings, pltpu.HBM),
        pltpu.with_memory_space_constraint(cluster_ids.reshape(1, ROWS), pltpu.HBM),
        pltpu.with_memory_space_constraint(order, pltpu.HBM),
    )
    got = lax.all_to_all(send, CHIP_AXES, split_axis=0, concat_axis=0, tiled=True)
    other = lax.ppermute(got, "c", [(0, 1), (1, 0)])
    cost = pl.CostEstimate(flops=2 * HALF * HALF * WIDTH, bytes_accessed=8 << 20, transcendentals=0)
    rows, query_late, best = pl.pallas_call(
        own_scores,
        out_shape=(shape((HALF, WIDTH), BF16), shape((1, HALF), F32), shape((8, HALF), F32)),
        scratch_shapes=[pltpu.VMEM((HALF, 128), F32)],
        compiler_params=PARAMS,
        cost_estimate=cost,
    )(got)
    back = pl.pallas_call(
        other_scores,
        out_shape=shape((2 * CHIPS, 1, 128), F32),
        compiler_params=PARAMS,
        cost_estimate=cost,
    )(other, rows, query_late, best)
    returned = lax.all_to_all(back, BACK_AXES, split_axis=0, concat_axis=0, tiled=True)
    return pl.pallas_call(
        finish,
        out_shape=shape((ROWS,), F32),
        compiler_params=PARAMS,
    )(returned, place)


def solution(mesh):
    fine = Mesh(mesh.devices.reshape(4, 4, PLANES, 2), AXES)
    return jax.shard_map(
        per_device,
        mesh=fine,
        in_specs=(P(AXES, None), P(AXES, None), P(AXES)),
        out_specs=P(AXES),
        check_vma=False,
    )
```

```python
import jax
import jax.numpy as jnp
from jax import lax
from jax.experimental import pallas as pl
from jax.experimental.pallas import tpu as pltpu
from jax.sharding import Mesh, PartitionSpec as P

CLUSTERS = 48
MOST = 24
WIDTH = 1024
ROWS = 384
CHIPS = 64
PLANES = 4
USED = 3
BLOCKS = WIDTH // 128
CHUNK = BLOCKS * MOST + 8
HALF = CHIPS * MOST
TILE = 32 * MOST
TOP = 65535
LOW = 64
PIECES = 3
PARTS = 3
THIRD = 32
F32 = jnp.float32
BF16 = jnp.bfloat16
AXES = ("x", "y", "z", "c")
CHIP_AXES = ("x", "y", "z")
BACK_AXES = ("c", "x", "y", "z")


def iota(shape, dim):
    return lax.broadcasted_iota(jnp.int32, shape, dim)


def chunk_of(cluster):
    return cluster // USED * PLANES + cluster % USED


def prepare(
    emb_hbm, cluster_hbm, order_hbm, send_ref, place_ref,
    emb_ref, cluster_ref, order_ref, sem,
):
    copies = [
        pltpu.make_async_copy(cluster_hbm, cluster_ref, sem.at[PIECES]),
        pltpu.make_async_copy(order_hbm, order_ref, sem.at[PIECES + 1]),
    ]
    piece = ROWS // PIECES
    for one in range(PIECES):
        rows = pl.ds(one * piece, piece)
        copies.append(
            pltpu.make_async_copy(emb_hbm.at[rows, :], emb_ref.at[rows, :], sem.at[one])
        )
    for copy in copies:
        copy.start()
    for unused in range(USED, CHIPS, PLANES):
        send_ref[unused] = jnp.zeros((CHUNK, 128), BF16)
    before = (iota((ROWS, ROWS), 0) < iota((ROWS, ROWS), 1)).astype(BF16)
    copies[0].wait()
    copies[1].wait()
    cluster = cluster_ref[...]
    hot = (iota((CLUSTERS, ROWS), 0) == cluster).astype(BF16)
    counts = jnp.dot(hot, before, preferred_element_type=F32)
    rank = jnp.sum(counts * hot.astype(F32), axis=0, keepdims=True).astype(jnp.int32)
    slot = cluster * MOST + rank
    place_ref[0:1, :] = cluster + ((cluster * 171) >> 9)
    place_ref[1:2, :] = rank

    late = TOP - order_ref[...].reshape(1, ROWS)
    high = (late >> 8).astype(F32)
    low = (late & 255).astype(F32)
    lane = iota((128, ROWS), 0)
    coded = jnp.where(lane == rank, high, 0.0) + jnp.where(lane == rank + LOW, low, 0.0)
    orders = lax.dot_general(
        hot, coded.astype(BF16), (((1,), (1,)), ((), ())), preferred_element_type=F32
    )

    units = []
    for one in range(PIECES):
        copies[2 + one].wait()
        emb = emb_ref[one * piece : (one + 1) * piece, :]
        total = jnp.sum(emb * emb, axis=1, keepdims=True)
        units.append((emb * lax.rsqrt(total + 1e-06)).astype(BF16))
    unit = jnp.concatenate(units, axis=0)
    step = CLUSTERS // PARTS
    for part in range(PARTS):
        rows = step * MOST
        pick = (iota((rows, ROWS), 0) + part * rows == slot).astype(BF16)
        taken = jnp.dot(pick, unit, preferred_element_type=F32).astype(BF16)
        for one in range(step):
            cluster_id = part * step + one
            to = chunk_of(cluster_id)
            for block in range(BLOCKS):
                send_ref[to, block * MOST : (block + 1) * MOST, :] = taken[
                    one * MOST : (one + 1) * MOST, block * 128 : (block + 1) * 128
                ]
            send_ref[to, BLOCKS * MOST : CHUNK, :] = jnp.broadcast_to(
                orders[cluster_id : cluster_id + 1, :], (8, 128)
            ).astype(BF16)


def key_lateness(got_ref, first, count):
    tile = got_ref[first : first + count, BLOCKS * MOST : CHUNK, :].astype(F32)
    row = iota((1, 8, 128), 1)
    lane = iota((1, 8, 128), 2)
    parts = []
    for start in range(0, MOST, 8):
        weight = jnp.where(lane == row + start, 256.0, 0.0)
        weight = weight + jnp.where(lane == row + (start + LOW), 1.0, 0.0)
        parts.append(tile * weight)
    wide = jnp.concatenate(parts, axis=1).reshape(count * MOST, 128)
    return jnp.sum(wide, axis=1, keepdims=True)


def unpacked(got_ref, first):
    rows = TILE // MOST
    return jnp.concatenate(
        [
            got_ref[
                first * rows : (first + 1) * rows, block * MOST : (block + 1) * MOST, :
            ].reshape(TILE, 128)
            for block in range(BLOCKS)
        ],
        axis=1,
    )


def fold(scores):
    rows, columns = scores.shape
    return jnp.max(scores.reshape(rows // 8, 8, columns), axis=0)


def score(keys, queries):
    return lax.dot_general(
        keys, queries, (((1,), (1,)), ((), ())), preferred_element_type=F32
    )


def own_scores(got_ref, rows_ref, query_late_ref, best_ref, late_ref):
    for part in range(HALF // TILE):
        rows_ref[part * TILE : (part + 1) * TILE, :] = unpacked(got_ref, part)
    late_ref[...] = jnp.broadcast_to(key_lateness(got_ref, 0, CHIPS), (HALF, 128))
    query_late = jnp.transpose(late_ref[...])[0:1, :]
    query_late_ref[...] = query_late
    best = jnp.full((8, HALF), -1.0, F32)
    for part in range(HALF // TILE):
        rows = slice(part * TILE, (part + 1) * TILE)
        scores = score(rows_ref[rows, :], rows_ref[...])
        kept = jnp.where(late_ref[rows, 0:1] > query_late, scores, -1.0)
        best = jnp.maximum(best, fold(kept))
    best_ref[...] = best


def exact_parts(values):
    high = values.astype(BF16)
    rest = values - high.astype(F32)
    middle = rest.astype(BF16)
    low = (rest - middle.astype(F32)).astype(BF16)
    return high, middle, low


def by_source(best):
    sources = TILE // MOST
    column = iota((sources, TILE), 1)
    source = iota((sources, TILE), 0) * MOST
    member = (column >= source) & (column < source + MOST)
    row = jnp.sum(jnp.where(member, column - source, 0), axis=0, keepdims=True)
    here = iota((THIRD, TILE), 0) == row
    member = member.astype(F32).astype(BF16)
    none = jnp.zeros((THIRD, TILE), F32)
    groups = []
    for start in range(0, HALF, TILE):
        values = exact_parts(best[:, start : start + TILE])
        spread = [jnp.where(here, one.astype(F32), 0.0) for one in values]
        parts = lax.dot_general(
            member,
            jnp.concatenate(spread + [none], axis=0).astype(BF16),
            (((1,), (1,)), ((), ())),
            preferred_element_type=F32,
        )
        groups.append(
            (pltpu.roll(parts, 2 * THIRD, 1) + pltpu.roll(parts, 3 * THIRD, 1)) + parts
        )
    return jnp.concatenate(groups, axis=0)


def cross(got_ref, rows_ref, query_late_ref, best_ref, back_ref, first, queries, own_at, other_at):
    sources = TILE // MOST
    best = best_ref[:, 0:queries]
    query_late = query_late_ref[:, 0:queries]
    if first:
        back_ref[other_at : other_at + first] = jnp.full((first, 1, 128), -1.0, F32)
    for source in range(first, CHIPS, sources):
        scores = score(unpacked(got_ref, source // sources), rows_ref[0:queries, :])
        later = key_lateness(got_ref, source, sources) > query_late
        best = jnp.maximum(best, fold(jnp.where(later, scores, -1.0)))
        turned = jnp.where(later, -1.0, scores)
        wide = turned[:, 0:128]
        for start in range(128, queries, 128):
            wide = jnp.maximum(wide, turned[:, start : start + 128])
        found = jnp.max(wide, axis=1, keepdims=True)
        found = jnp.broadcast_to(found, (TILE, 128)).reshape(sources, MOST, 128)
        shape = (sources, MOST, 128)
        placed = jnp.where(iota(shape, 1) == iota(shape, 2), found, 0.0)
        back_ref[other_at + source : other_at + source + sources] = jnp.sum(
            placed, axis=1
        ).reshape(sources, 1, 128)
    if queries < HALF:
        best = jnp.concatenate([best, best_ref[:, queries:HALF]], axis=1)
    best = jnp.max(best, axis=0, keepdims=True)
    back_ref[own_at : own_at + CHIPS] = by_source(best).reshape(CHIPS, 1, 128)


def other_scores(got_ref, rows_ref, query_late_ref, best_ref, back_ref):
    core = lax.axis_index("c")
    refs = (got_ref, rows_ref, query_late_ref, best_ref, back_ref)

    @pl.when(core == 0)
    def _():
        cross(*refs, first=0, queries=HALF // 2, own_at=0, other_at=CHIPS)

    @pl.when(core == 1)
    def _():
        cross(*refs, first=CHIPS // 2, queries=HALF, own_at=CHIPS, other_at=0)


def finish(back_ref, place_ref, out_ref):
    back = jnp.maximum(back_ref[0:CHIPS], back_ref[CHIPS : 2 * CHIPS]).reshape(CHIPS, 128)
    member = (iota((CHIPS, ROWS), 0) == place_ref[0:1, :]).astype(BF16)
    columns = lax.dot_general(
        jnp.concatenate(exact_parts(back), axis=0),
        jnp.concatenate([member, member, member], axis=0),
        (((0,), (0,)), ((), ())),
        preferred_element_type=F32,
    )
    here = iota((THIRD, ROWS), 0) == place_ref[1:2, :]
    out_ref[...] = jnp.sum(jnp.where(here, columns[0:THIRD, :], 0.0), axis=0)


PARAMS = pltpu.CompilerParams(vmem_limit_bytes=24 * 1024 * 1024)


def per_device(embeddings, cluster_ids, order):
    shape = jax.ShapeDtypeStruct
    send, place = pl.pallas_call(
        prepare,
        out_shape=(shape((CHIPS, CHUNK, 128), BF16), shape((2, ROWS), jnp.int32)),
        in_specs=[pl.BlockSpec(memory_space=pltpu.HBM)] * 3,
        scratch_shapes=[
            pltpu.VMEM((ROWS, WIDTH), F32),
            pltpu.VMEM((1, ROWS), jnp.int32),
            pltpu.VMEM((ROWS,), jnp.int32),
            pltpu.SemaphoreType.DMA((PIECES + 2,)),
        ],
        compiler_params=pltpu.CompilerParams(vmem_limit_bytes=24 * 1024 * 1024),
    )(
        pltpu.with_memory_space_constraint(embeddings, pltpu.HBM),
        pltpu.with_memory_space_constraint(cluster_ids.reshape(1, ROWS), pltpu.HBM),
        pltpu.with_memory_space_constraint(order, pltpu.HBM),
    )
    got = lax.all_to_all(send, CHIP_AXES, split_axis=0, concat_axis=0, tiled=True)
    other = lax.ppermute(got, "c", [(0, 1), (1, 0)])
    cost = pl.CostEstimate(flops=2 * HALF * HALF * WIDTH, bytes_accessed=8 << 20, transcendentals=0)
    rows, query_late, best = pl.pallas_call(
        own_scores,
        out_shape=(shape((HALF, WIDTH), BF16), shape((1, HALF), F32), shape((8, HALF), F32)),
        scratch_shapes=[pltpu.VMEM((HALF, 128), F32)],
        compiler_params=PARAMS,
        cost_estimate=cost,
    )(got)
    back = pl.pallas_call(
        other_scores,
        out_shape=shape((2 * CHIPS, 1, 128), F32),
        compiler_params=PARAMS,
        cost_estimate=cost,
    )(other, rows, query_late, best)
    returned = lax.all_to_all(back, BACK_AXES, split_axis=0, concat_axis=0, tiled=True)
    return pl.pallas_call(
        finish,
        out_shape=shape((ROWS,), F32),
        compiler_params=PARAMS,
    )(returned, place)


def solution(mesh):
    fine = Mesh(mesh.devices.reshape(4, 4, PLANES, 2), AXES)
    return jax.shard_map(
        per_device,
        mesh=fine,
        in_specs=(P(AXES, None), P(AXES, None), P(AXES)),
        out_specs=P(AXES),
        check_vma=False,
    )
```

```python
import jax
import jax.numpy as jnp
from jax import lax
from jax.experimental import pallas as pl
from jax.experimental.pallas import tpu as pltpu
from jax.sharding import Mesh, PartitionSpec as P

CLUSTERS = 48
MOST = 24
WIDTH = 1024
ROWS = 384
CHIPS = 64
PLANES = 4
USED = 3
BLOCKS = WIDTH // 128
CHUNK = BLOCKS * MOST + 8
HALF = CHIPS * MOST
TILE = 32 * MOST
TOP = 65535
LOW = 64
PIECES = 3
PARTS = 3
THIRD = 32
F32 = jnp.float32
BF16 = jnp.bfloat16
AXES = ("x", "y", "z", "c")
CHIP_AXES = ("x", "y", "z")
BACK_AXES = ("c", "x", "y", "z")


def iota(shape, dim):
    return lax.broadcasted_iota(jnp.int32, shape, dim)


def chunk_of(cluster):
    return cluster // USED * PLANES + cluster % USED


def prepare(
    emb_hbm, cluster_hbm, order_hbm, send_ref, place_ref,
    emb_ref, cluster_ref, order_ref, sem,
):
    copies = [
        pltpu.make_async_copy(cluster_hbm, cluster_ref, sem.at[PIECES]),
        pltpu.make_async_copy(order_hbm, order_ref, sem.at[PIECES + 1]),
    ]
    piece = ROWS // PIECES
    for one in range(PIECES):
        rows = pl.ds(one * piece, piece)
        copies.append(
            pltpu.make_async_copy(emb_hbm.at[rows, :], emb_ref.at[rows, :], sem.at[one])
        )
    for copy in copies:
        copy.start()
    for unused in range(USED, CHIPS, PLANES):
        send_ref[unused] = jnp.zeros((CHUNK, 128), BF16)
    before = (iota((ROWS, ROWS), 0) < iota((ROWS, ROWS), 1)).astype(BF16)
    copies[0].wait()
    copies[1].wait()
    cluster = cluster_ref[...]
    hot = (iota((CLUSTERS, ROWS), 0) == cluster).astype(BF16)
    counts = jnp.dot(hot, before, preferred_element_type=F32)
    rank = jnp.sum(counts * hot.astype(F32), axis=0, keepdims=True).astype(jnp.int32)
    slot = cluster * MOST + rank
    place_ref[0:1, :] = cluster + ((cluster * 171) >> 9)
    place_ref[1:2, :] = rank

    late = TOP - order_ref[...].reshape(1, ROWS)
    high = (late >> 8).astype(F32)
    low = (late & 255).astype(F32)
    lane = iota((128, ROWS), 0)
    coded = jnp.where(lane == rank, high, 0.0) + jnp.where(lane == rank + LOW, low, 0.0)
    orders = lax.dot_general(
        hot, coded.astype(BF16), (((1,), (1,)), ((), ())), preferred_element_type=F32
    )

    for cluster_id in range(CLUSTERS):
        send_ref[chunk_of(cluster_id), BLOCKS * MOST : CHUNK, :] = jnp.broadcast_to(
            orders[cluster_id : cluster_id + 1, :], (8, 128)
        ).astype(BF16)
    rows = CLUSTERS // PARTS * MOST
    picks = [(iota((rows, ROWS), 0) == slot).astype(BF16)]
    units = []
    for one in range(PIECES):
        copies[2 + one].wait()
        emb = emb_ref[one * piece : (one + 1) * piece, :]
        total = jnp.sum(emb * emb, axis=1, keepdims=True)
        units.append((emb * lax.rsqrt(total + 1e-06)).astype(BF16))
    unit = jnp.concatenate(units, axis=0)
    step = CLUSTERS // PARTS
    for part in range(PARTS):
        rows = step * MOST
        if part:
            picks.append((iota((rows, ROWS), 0) + part * rows == slot).astype(BF16))
        taken = jnp.dot(picks[part], unit, preferred_element_type=F32).astype(BF16)
        for one in range(step):
            cluster_id = part * step + one
            to = chunk_of(cluster_id)
            for block in range(BLOCKS):
                send_ref[to, block * MOST : (block + 1) * MOST, :] = taken[
                    one * MOST : (one + 1) * MOST, block * 128 : (block + 1) * 128
                ]


def key_lateness(got_ref, first, count):
    tile = got_ref[first : first + count, BLOCKS * MOST : CHUNK, :].astype(F32)
    row = iota((1, 8, 128), 1)
    lane = iota((1, 8, 128), 2)
    parts = []
    for start in range(0, MOST, 8):
        weight = jnp.where(lane == row + start, 256.0, 0.0)
        weight = weight + jnp.where(lane == row + (start + LOW), 1.0, 0.0)
        parts.append(tile * weight)
    wide = jnp.concatenate(parts, axis=1).reshape(count * MOST, 128)
    return jnp.sum(wide, axis=1, keepdims=True)


def unpacked(got_ref, first):
    rows = TILE // MOST
    return jnp.concatenate(
        [
            got_ref[
                first * rows : (first + 1) * rows, block * MOST : (block + 1) * MOST, :
            ].reshape(TILE, 128)
            for block in range(BLOCKS)
        ],
        axis=1,
    )


def fold(scores):
    rows, columns = scores.shape
    return jnp.max(scores.reshape(rows // 8, 8, columns), axis=0)


def score(keys, queries):
    return lax.dot_general(
        keys, queries, (((1,), (1,)), ((), ())), preferred_element_type=F32
    )


def own_scores(got_ref, rows_ref, query_late_ref, best_ref, late_ref):
    for part in range(HALF // TILE):
        rows_ref[part * TILE : (part + 1) * TILE, :] = unpacked(got_ref, part)
    late_ref[...] = jnp.broadcast_to(key_lateness(got_ref, 0, CHIPS), (HALF, 128))
    query_late = jnp.transpose(late_ref[...])[0:1, :]
    query_late_ref[...] = query_late
    best = jnp.full((8, HALF), -1.0, F32)
    for part in range(HALF // TILE):
        rows = slice(part * TILE, (part + 1) * TILE)
        scores = score(rows_ref[rows, :], rows_ref[...])
        kept = jnp.where(late_ref[rows, 0:1] > query_late, scores, -1.0)
        best = jnp.maximum(best, fold(kept))
    best_ref[...] = best


def exact_parts(values):
    high = values.astype(BF16)
    rest = values - high.astype(F32)
    middle = rest.astype(BF16)
    low = (rest - middle.astype(F32)).astype(BF16)
    return high, middle, low


def by_source(best):
    sources = TILE // MOST
    column = iota((sources, TILE), 1)
    source = iota((sources, TILE), 0) * MOST
    member = (column >= source) & (column < source + MOST)
    row = jnp.sum(jnp.where(member, column - source, 0), axis=0, keepdims=True)
    here = iota((THIRD, TILE), 0) == row
    member = member.astype(F32).astype(BF16)
    none = jnp.zeros((THIRD, TILE), F32)
    groups = []
    for start in range(0, HALF, TILE):
        values = exact_parts(best[:, start : start + TILE])
        spread = [jnp.where(here, one.astype(F32), 0.0) for one in values]
        parts = lax.dot_general(
            member,
            jnp.concatenate(spread + [none], axis=0).astype(BF16),
            (((1,), (1,)), ((), ())),
            preferred_element_type=F32,
        )
        groups.append(
            (pltpu.roll(parts, 2 * THIRD, 1) + pltpu.roll(parts, 3 * THIRD, 1)) + parts
        )
    return jnp.concatenate(groups, axis=0)


def cross(got_ref, rows_ref, query_late_ref, best_ref, back_ref, first, queries, own_at, other_at):
    sources = TILE // MOST
    starts = range(0, HALF, TILE)
    best = [best_ref[:, start : start + TILE] for start in starts]
    if first:
        back_ref[other_at : other_at + first] = jnp.full((first, 1, 128), -1.0, F32)
    for source in range(first, CHIPS, sources):
        keys = unpacked(got_ref, source // sources)
        late = key_lateness(got_ref, source, sources)
        wide = jnp.full((TILE, 128), -1.0, F32)
        for number in range(queries // TILE):
            columns = slice(number * TILE, (number + 1) * TILE)
            scores = score(keys, rows_ref[columns, :])
            later = late > query_late_ref[:, columns]
            best[number] = jnp.maximum(best[number], fold(jnp.where(later, scores, -1.0)))
            turned = jnp.where(later, -1.0, scores)
            for start in range(0, TILE, 128):
                wide = jnp.maximum(wide, turned[:, start : start + 128])
        found = jnp.max(wide, axis=1, keepdims=True)
        shape = (sources, MOST, 128)
        found = jnp.broadcast_to(found, (TILE, 128)).reshape(shape)
        placed = jnp.where(iota(shape, 1) == iota(shape, 2), found, 0.0)
        back_ref[other_at + source : other_at + source + sources] = jnp.sum(
            placed, axis=1
        ).reshape(sources, 1, 128)
    best = jnp.max(jnp.concatenate(best, axis=1), axis=0, keepdims=True)
    back_ref[own_at : own_at + CHIPS] = by_source(best).reshape(CHIPS, 1, 128)


def other_scores(got_ref, rows_ref, query_late_ref, best_ref, back_ref):
    core = lax.axis_index("c")
    refs = (got_ref, rows_ref, query_late_ref, best_ref, back_ref)

    @pl.when(core == 0)
    def _():
        cross(*refs, first=0, queries=HALF // 2, own_at=0, other_at=CHIPS)

    @pl.when(core == 1)
    def _():
        cross(*refs, first=CHIPS // 2, queries=HALF, own_at=CHIPS, other_at=0)


def finish(back_ref, place_ref, out_ref):
    back = jnp.maximum(back_ref[0:CHIPS], back_ref[CHIPS : 2 * CHIPS]).reshape(CHIPS, 128)
    member = (iota((CHIPS, ROWS), 0) == place_ref[0:1, :]).astype(BF16)
    turned = jnp.transpose(back)[0:THIRD, :]
    columns = jnp.dot(
        jnp.concatenate(exact_parts(turned), axis=1),
        jnp.concatenate([member, member, member], axis=0),
        preferred_element_type=F32,
    )
    here = iota((THIRD, ROWS), 0) == place_ref[1:2, :]
    out_ref[...] = jnp.sum(jnp.where(here, columns[0:THIRD, :], 0.0), axis=0)


PARAMS = pltpu.CompilerParams(vmem_limit_bytes=24 * 1024 * 1024)


def per_device(embeddings, cluster_ids, order):
    shape = jax.ShapeDtypeStruct
    send, place = pl.pallas_call(
        prepare,
        out_shape=(shape((CHIPS, CHUNK, 128), BF16), shape((2, ROWS), jnp.int32)),
        in_specs=[pl.BlockSpec(memory_space=pltpu.HBM)] * 3,
        scratch_shapes=[
            pltpu.VMEM((ROWS, WIDTH), F32),
            pltpu.VMEM((1, ROWS), jnp.int32),
            pltpu.VMEM((ROWS,), jnp.int32),
            pltpu.SemaphoreType.DMA((PIECES + 2,)),
        ],
        compiler_params=pltpu.CompilerParams(vmem_limit_bytes=24 * 1024 * 1024),
    )(
        pltpu.with_memory_space_constraint(embeddings, pltpu.HBM),
        pltpu.with_memory_space_constraint(cluster_ids.reshape(1, ROWS), pltpu.HBM),
        pltpu.with_memory_space_constraint(order, pltpu.HBM),
    )
    got = lax.all_to_all(send, CHIP_AXES, split_axis=0, concat_axis=0, tiled=True)
    other = lax.ppermute(got, "c", [(0, 1), (1, 0)])
    cost = pl.CostEstimate(flops=2 * HALF * HALF * WIDTH, bytes_accessed=8 << 20, transcendentals=0)
    rows, query_late, best = pl.pallas_call(
        own_scores,
        out_shape=(shape((HALF, WIDTH), BF16), shape((1, HALF), F32), shape((8, HALF), F32)),
        scratch_shapes=[pltpu.VMEM((HALF, 128), F32)],
        compiler_params=PARAMS,
        cost_estimate=cost,
    )(got)
    back = pl.pallas_call(
        other_scores,
        out_shape=shape((2 * CHIPS, 1, 128), F32),
        compiler_params=PARAMS,
        cost_estimate=cost,
    )(other, rows, query_late, best)
    returned = lax.all_to_all(back, BACK_AXES, split_axis=0, concat_axis=0, tiled=True)
    return pl.pallas_call(
        finish,
        out_shape=shape((ROWS,), F32),
        compiler_params=PARAMS,
    )(returned, place)


def solution(mesh):
    fine = Mesh(mesh.devices.reshape(4, 4, PLANES, 2), AXES)
    return jax.shard_map(
        per_device,
        mesh=fine,
        in_specs=(P(AXES, None), P(AXES, None), P(AXES)),
        out_specs=P(AXES),
        check_vma=False,
    )
```
